128 devices in a mesh: batch: 4 (over x_lo, core), label: 32 (over z, x_hi, y).
Axes of the slice: x: 4 (x_hi: 2, x_lo: 2; x = x_hi * 2 + x_lo), y: 4, z: 4, core: 2. Of those that a mesh axis runs over, the one named last changes fastest.
Arguments:
- encoded: bfloat16 [4096, 768], P(('batch', 'label')), may hold values from -6 to 6
- label_ids: int32 [4096, 32], P(('batch', 'label')), may hold values from -1 to 131071, as said below
- weights: float32 [131072, 768], P(('batch', 'label')), may hold values from -0.21875 to 0.21875
- accum: float32 [131072, 768], P(('batch', 'label')), may hold values from 1 to 4096
Outputs:
- encoder_grad: bfloat16 [4096, 768], P(('batch', 'label'))
- new_weights: float32 [131072, 768], P(('batch', 'label'))
- new_accum: float32 [131072, 768], P(('batch', 'label'))
The draws below stay inside these ranges and needn't reach their ends.
Inputs may be any that keep to these rules, and one draw needn't show every extreme that they name: `label_ids`: each row holds its valid ids in its first slots and -1 after them, at least one valid id; the valid ids of a row are distinct.
All inputs are finite; a program needn't handle non-finite values.
Results may differ from the reference program's by a relative error of at most 0.0098.
Values may be sent and summed in bfloat16 or wider, within the bound.
A program may use at most 128 MiB of HBM per device.

```python
import math
import jax
import jax.numpy as jnp
from jax import lax

D = 768
SLOTS = 32
LR_DEV = 1024
SAMPLES = 4096
LABELS = 131072
N_BATCH = 4
N_LABEL = 32


def draw_label_ids(key, part):
    key = jax.random.fold_in(key, 7)
    key_base, key_count, key_order = jax.random.split(key, 3)
    base = jax.random.randint(key_base, (SAMPLES, SLOTS), 0, LABELS - SLOTS + 1)
    base = jnp.sort(base, axis=1)
    base = base.at[0, SLOTS - 1].set(LABELS - SLOTS)
    slot = jnp.arange(SLOTS, dtype=jnp.int32)[None, :]
    ids = (base + slot).astype(jnp.int32)
    scores = jax.random.randint(key_order, (SAMPLES, SLOTS), 0, 1 << 20) * SLOTS + slot
    order = jnp.argsort(scores, axis=1).astype(jnp.int32)
    ids = jnp.take_along_axis(ids, order, axis=1)
    count = jax.random.randint(key_count, (SAMPLES, 1), 1, SLOTS + 1)
    count = count.at[0, 0].set(SLOTS).at[1, 0].set(1)
    return jnp.where(slot < count, ids, -1).astype(jnp.int32)


def level_of(stream_key, shape, cuts, smallest, largest):
    def one(dim, blocks):
        draws = jax.random.uniform(jax.random.fold_in(jax.random.fold_in(stream_key, 6), dim), (blocks,), jnp.float32, smallest / len(cuts), largest / len(cuts))
        return jnp.repeat(jnp.exp(draws), shape[dim] // blocks).reshape((-1,) + (1,) * (len(shape) - dim - 1))

    gain = one(*cuts[0])
    for cut in cuts[1:]:
        gain = gain * one(*cut)
    return gain


def gaussian(stream_key, dims, scale, bound, cuts=(), kind=jnp.bfloat16):
    values = jax.random.normal(stream_key, dims, jnp.float32) * scale
    if len(cuts) > 0:
        values = level_of(stream_key, dims, cuts, -0.22, 0.18) * values
    return jnp.clip(values, min=-bound, max=bound).astype(kind)


def setup_inputs(seed: int = 0) -> dict:
    seeds = jax.random.split(jax.random.key(seed), 5)
    encoded = gaussian(seeds[0], (SAMPLES, D), 1.0, 6.0, ((0, 128),))
    label_ids = draw_label_ids(jax.random.fold_in(seeds[4], 71), 0)
    weights = gaussian(seeds[2], (LABELS, D), D ** -0.5, 0.21875, ((0, 128),), jnp.float32)
    accum = jnp.clip(jnp.exp(math.log(4096.0) - 8.317766 * jax.random.uniform(seeds[3], (LABELS, D), jnp.float32) ** level_of(seeds[3], (LABELS, D), ((0, 128),), -0.2, 0.2)), 1.0, 4096.0)
    return {"encoded": encoded, "label_ids": label_ids, "weights": weights, "accum": accum}


def reference(encoded, label_ids, weights, accum):
    shards = N_BATCH * N_LABEL
    w_blocks = weights.reshape(shards, LR_DEV, D)
    a_blocks = accum.reshape(shards, LR_DEV, D)
    starts = jnp.arange(shards, dtype=jnp.int32) * LR_DEV
    row_index = jnp.arange(SAMPLES, dtype=jnp.int32)[:, None]

    def step(carry, inputs):
        w_block, a_block, start = inputs
        w_low = w_block.astype(jnp.bfloat16)
        logits = jnp.dot(encoded, w_low.T, preferred_element_type=jnp.float32)
        local = label_ids - start
        valid = (label_ids >= 0) & (local >= 0) & (local < LR_DEV)
        column = jnp.where(valid, local, LR_DEV).astype(jnp.int32)
        prob = jax.nn.sigmoid(logits)
        prob = prob.at[row_index, column].add(-1.0, mode='drop')
        delta = prob.astype(jnp.bfloat16)
        grad = jnp.dot(delta.T, encoded, preferred_element_type=jnp.float32)
        carry = carry + jnp.dot(delta, w_low, preferred_element_type=jnp.float32)
        new_a = a_block + grad * grad
        new_w = w_block - 0.5 * grad / jnp.sqrt(new_a)
        return (carry, (new_w, new_a))
    init = jnp.zeros((SAMPLES, D), jnp.float32)
    total, (new_w, new_a) = lax.scan(step, init, (w_blocks, a_blocks, starts))
    return (total.astype(jnp.bfloat16), new_w.reshape(LABELS, D), new_a.reshape(LABELS, D))
```

```python
import functools

import jax
import jax.numpy as jnp
from jax import lax
from jax.experimental import pallas as pl
from jax.experimental.pallas import tpu as pltpu
from jax.sharding import PartitionSpec as P

MESH = pl.DeviceIdType.MESH
NT = (((1,), (1,)), ((), ()))
TN = (((0,), (0,)), ((), ()))
GATHER_ORDER = ((0, 1, 2), (1, 2, 0), (2, 0, 1), (0, 1, 2))
SCATTER_ORDER = ((0, 1, 2), (1, 2, 0), (2, 0, 1))
F32 = jnp.float32
BF16 = jnp.bfloat16


def place(n):
    batch, label = lax.axis_index("batch"), lax.axis_index("label")
    core = lax.rem(batch, 2)
    x = lax.rem(lax.div(label, n), n // 2) * 2 + lax.div(batch, 2)
    y = lax.rem(label, n)
    z = lax.div(label, n * (n // 2))
    return (x, y, z), core


def device(n, xyz, core):
    x, y, z = xyz
    return (
        lax.rem(x, 2) * 2 + core,
        z * (n * (n // 2)) + lax.div(x, 2) * n + y,
    )


def kernel(
    n, enc_ref, ids_ref, w_ref, out_ref, grad_ref,
    rows, ids, w_wide, w_low, mask, delta, part, from_core, recv1, sum2, recv2, sum3, recv3, pad,
    w_sem, g_send, g_recv, c_send, c_recv, x_send, x_recv, s_send, s_recv,
):
    me, core = place(n)
    other = 1 - core
    labels = w_ref.shape[0]
    batch, label = lax.axis_index("batch"), lax.axis_index("label")
    offset = (batch * lax.axis_size("label") + label) * labels
    sibling = device(n, me, other)

    def shifted(axis, by):
        return tuple(lax.rem(me[a] + by, n) if a == axis else me[a] for a in range(3))

    w_copy = pltpu.make_async_copy(w_ref, w_wide, w_sem)
    w_copy.start()

    barrier = pltpu.get_barrier_semaphore()
    for axis in range(3):
        for by in range(1, n):
            pl.semaphore_signal(
                barrier, inc=1, device_id=device(n, shifted(axis, by), core), device_id_type=MESH
            )
    pl.semaphore_signal(barrier, inc=1, device_id=sibling, device_id_type=MESH)

    for j in range(3):
        rows[(j, core) + me] = enc_ref[:, j * 256 : (j + 1) * 256]
    pad[:, 0:32] = ids_ref[...]
    lane8 = lax.broadcasted_iota(jnp.int32, (8, 128), 1)
    turned = jnp.concatenate([pad[...]] * 4, axis=0).T
    packed = turned[0:8]
    for q in range(1, 4):
        packed = jnp.where(lax.shift_right_logical(lane8, 5) == q, turned[8 * q : 8 * q + 8], packed)
    ids[(core,) + me] = packed

    pl.semaphore_wait(barrier, 3 * (n - 1) + 1)

    def gathered(j, index):
        return rows.at[(j, core) + index] if j < 3 else ids.at[(core,) + index]

    def g_copy(j, step, by):
        order = GATHER_ORDER[j]
        index = tuple(slice(None) if a in order[:step] else me[a] for a in range(3))
        ref = gathered(j, index)
        return pltpu.make_async_remote_copy(
            src_ref=ref, dst_ref=ref,
            send_sem=g_send.at[j, step, by - 1], recv_sem=g_recv.at[j, step, by - 1],
            device_id=device(n, shifted(order[step], by), core), device_id_type=MESH,
        )

    def c_copy(j, by):
        last = GATHER_ORDER[j][2]
        plane = lax.rem(me[last] + n - by, n)
        ref = gathered(j, tuple(plane if a == last else slice(None) for a in range(3)))
        return pltpu.make_async_remote_copy(
            src_ref=ref, dst_ref=ref, send_sem=c_send.at[j, by], recv_sem=c_recv.at[j, by],
            device_id=sibling, device_id_type=MESH,
        )

    pieces = (3, 0, 1, 2)
    for step in range(3):
        for j in pieces:
            if step > 0:
                for by in range(1, n):
                    g_copy(j, step - 1, by).wait_recv()
            for by in range(1, n):
                g_copy(j, step, by).start()
            if step == 2:
                c_copy(j, 0).start()

    w_copy.wait()

    def narrow(i, _):
        at = pl.ds(pl.multiple_of(i * 128, 128), 128)
        for j in range(3):
            w_low[j, at, :] = w_wide[at, j * 256 : (j + 1) * 256].astype(BF16)
        return 0

    lax.fori_loop(0, labels // 128, narrow, 0)

    for by in range(1, n):
        for j in pieces:
            g_copy(j, 2, by).wait_recv()
            c_copy(j, by).start()
    for by in range(n):
        for j in pieces:
            c_copy(j, by).wait_recv()

    sub8 = lax.broadcasted_iota(jnp.int32, (8, 128), 0)
    lane_all = lax.broadcasted_iota(jnp.int32, (128, 128), 1)

    def mask_block(cx, _):
        four = ids[lax.div(cx, n), lax.rem(cx, n)].reshape(n * n, 8, 128)
        for g in range(n * n // 4):
            total = [None] * 4
            for q in range(4):
                local = four[4 * g + q] - offset
                valid = (local >= 0) & (local < labels)
                word = jnp.where(valid, local & 31, -1)
                bit = jnp.left_shift(jnp.int32(1), lax.shift_right_arithmetic(local, 5) & 31)
                held = [None] * 4
                for r in range(8):
                    word_r = jnp.broadcast_to(word[r : r + 1], (8, 128))
                    bit_r = jnp.broadcast_to(bit[r : r + 1], (8, 128))
                    for v in range(4):
                        hit = jnp.where(word_r == sub8 + 8 * v, bit_r, 0)
                        held[v] = hit if held[v] is None else held[v] | hit
                for v in range(4):
                    a = held[v] | pltpu.roll(held[v], 32, 1)
                    a = a | pltpu.roll(a, 64, 1)
                    total[v] = a if q == 0 else jnp.where(lax.shift_right_logical(lane8, 5) == q, a, total[v])
            bits = jnp.concatenate(total * 4, axis=0).T
            bits = lax.shift_right_logical(bits, lax.shift_right_logical(lane_all, 5))
            mask[cx, 4 * g : 4 * g + 4] = bits.reshape(4, 32, 128)
        return 0

    lax.fori_loop(0, 2 * n, mask_block, 0)

    tile = n * n * 16

    def half(h):
        return slice(16 * h, 16 * h + 16)

    def forward(h, c):
        def one(x, _):
            logits = None
            for j in range(3):
                e = rows[j, c, x, :, :, half(h), :].reshape(tile, 256)
                term = lax.dot_general(e, w_low[j], NT, preferred_element_type=F32)
                logits = term if logits is None else logits + term
            bits = mask[c * n + x, :, half(h), :].reshape(tile, 128)
            for t in range(labels // 128):
                sign = jnp.where((bits & (1 << (4 * t))) != 0, -1.0, 1.0)
                at = slice(128 * t, 128 * t + 128)
                delta[h, c, x, :, at] = (jnp.tanh(0.5 * logits[:, at]) + sign).astype(BF16)
            return 0

        lax.fori_loop(0, n, one, 0)

    def encoder_part(h, c, j):
        d = delta[h, c].reshape(n * tile, labels)
        r = jnp.dot(d, w_low[j], preferred_element_type=F32)
        part[j, h, c] = (0.5 * r).astype(BF16).reshape(n, n, n, 16, 256)

    def x_copy(j, h):
        return pltpu.make_async_remote_copy(
            src_ref=part.at[j, h, other], dst_ref=from_core.at[j, h],
            send_sem=x_send.at[j, h], recv_sem=x_recv.at[j, h],
            device_id=sibling, device_id_type=MESH,
        )

    def s_copy(j, h, step, by):
        order = SCATTER_ORDER[j]
        left = [a for a in range(3) if a not in order[:step]]
        to = shifted(order[step], by)
        index = tuple(to[a] if a == order[step] else slice(None) for a in left)
        src = (part.at[(j, h, core) + index], sum2.at[(j, h) + index], sum3.at[(j, h) + index])[step]
        dst = (recv1, recv2, recv3)[step].at[j, h, by - 1]
        return pltpu.make_async_remote_copy(
            src_ref=src, dst_ref=dst,
            send_sem=s_send.at[step, j, h, by - 1], recv_sem=s_recv.at[step, j, h, by - 1],
            device_id=device(n, to, core), device_id_type=MESH,
        )

    def own(j, h, step):
        order = SCATTER_ORDER[j]
        left = [a for a in range(3) if a not in order[:step]]
        index = tuple(me[a] if a == order[step] else slice(None) for a in left)
        ref = (part, sum2, sum3)[step]
        return ref[((j, h, core) if step == 0 else (j, h)) + index].astype(F32)

    def send(j, h, step):
        for by in range(1, n):
            s_copy(j, h, step, by).start()

    def add_core(h):
        for j in range(3):
            x_copy(j, h).wait_recv()

            def one(x, _):
                total = part[j, h, core, x].astype(F32) + from_core[j, h, x].astype(F32)
                part[j, h, core, x] = total.astype(BF16)
                return 0

            lax.fori_loop(0, n, one, 0)
            send(j, h, 0)

    def reduce(h, step):
        for j in range(3):
            for by in range(1, n):
                s_copy(j, h, step, by).wait_recv()
            total = own(j, h, step)
            for by in range(1, n):
                total = total + (recv1, recv2, recv3)[step][j, h, by - 1].astype(F32)
            if step == 2:
                out_ref[half(h), j * 256 : (j + 1) * 256] = total.astype(BF16)
            else:
                (sum2, sum3)[step][j, h] = total.astype(BF16)
                send(j, h, step + 1)

    def grad_part(t, j):
        at = slice(t * (labels // 2), (t + 1) * (labels // 2))
        total = None
        for h in range(2):
            for c in range(2):
                d = delta[h, c, :, :, at].reshape(n * tile, labels // 2)
                e = rows[j, c, :, :, :, half(h), :].reshape(n * tile, 256)
                term = lax.dot_general(d, e, TN, preferred_element_type=F32)
                total = term if total is None else total + term
        grad_ref[at, j * 256 : (j + 1) * 256] = 0.5 * total

    def block(h, c, send_it):
        forward(h, c)
        for j in range(3):
            encoder_part(h, c, j)
            if send_it:
                x_copy(j, h).start()

    block(0, other, True)
    block(0, core, False)
    add_core(0)
    block(1, other, True)
    reduce(0, 0)
    block(1, core, False)
    add_core(1)
    reduce(0, 1)
    grad_part(0, 0)
    grad_part(0, 1)
    reduce(0, 2)
    grad_part(0, 2)
    reduce(1, 0)
    grad_part(1, 0)
    reduce(1, 1)
    grad_part(1, 1)
    reduce(1, 2)
    grad_part(1, 2)

    for j in range(4):
        for step in range(3):
            for by in range(1, n):
                g_copy(j, step, by).wait_send()
        for by in range(n):
            c_copy(j, by).wait_send()
    for j in range(3):
        for h in range(2):
            x_copy(j, h).wait_send()
            for step in range(3):
                for by in range(1, n):
                    s_copy(j, h, step, by).wait_send()


def gradients(n, encoded, label_ids, weights):
    labels, width = weights.shape
    vmem = pltpu.VMEM
    dma = pltpu.SemaphoreType.DMA
    return pl.pallas_call(
        functools.partial(kernel, n),
        out_shape=(
            jax.ShapeDtypeStruct(encoded.shape, BF16),
            jax.ShapeDtypeStruct((labels, width), F32),
        ),
        in_specs=[
            pl.BlockSpec(memory_space=pltpu.VMEM),
            pl.BlockSpec(memory_space=pltpu.VMEM),
            pl.BlockSpec(memory_space=pl.ANY),
        ],
        out_specs=(
            pl.BlockSpec(memory_space=pltpu.VMEM),
            pl.BlockSpec(memory_space=pltpu.VMEM),
        ),
        scratch_shapes=[
            vmem((3, 2, n, n, n, 32, 256), BF16),
            vmem((2, n, n, n, 8, 128), jnp.int32),
            vmem((labels, width), F32),
            vmem((3, labels, 256), BF16),
            vmem((2 * n, n * n, 32, 128), jnp.int32),
            vmem((2, 2, n, n * n * 16, labels), BF16),
            vmem((3, 2, 2, n, n, n, 16, 256), BF16),
            vmem((3, 2, n, n, n, 16, 256), BF16),
            vmem((3, 2, n - 1, n, n, 16, 256), BF16),
            vmem((3, 2, n, n, 16, 256), BF16),
            vmem((3, 2, n - 1, n, 16, 256), BF16),
            vmem((3, 2, n, 16, 256), BF16),
            vmem((3, 2, n - 1, 16, 256), BF16),
            vmem((32, 128), jnp.int32),
            dma,
            dma((4, 3, n - 1)),
            dma((4, 3, n - 1)),
            dma((4, n)),
            dma((4, n)),
            dma((3, 2)),
            dma((3, 2)),
            dma((3, 3, 2, n - 1)),
            dma((3, 3, 2, n - 1)),
        ],
        compiler_params=pltpu.CompilerParams(
            collective_id=0, has_side_effects=True, vmem_limit_bytes=60 * 2**20
        ),
    )(encoded, label_ids, weights)


def on_device(n, encoded, label_ids, weights, accum):
    encoder_grad, grad = gradients(n, encoded, label_ids, weights)
    new_accum = accum + grad * grad
    new_weights = weights - 0.5 * grad / jnp.sqrt(new_accum)
    return (encoder_grad, new_weights, new_accum)


def solution(mesh):
    n = {4: 2, 32: 4}[mesh.shape["label"]]
    rows = P(("batch", "label"), None)
    return jax.shard_map(
        functools.partial(on_device, n),
        mesh=mesh,
        in_specs=(rows, rows, rows, rows),
        out_specs=(rows, rows, rows),
        check_vma=False,
    )
```

```python
import functools

import jax
import jax.numpy as jnp
from jax import lax
from jax.experimental import pallas as pl
from jax.experimental.pallas import tpu as pltpu
from jax.sharding import PartitionSpec as P

MESH = pl.DeviceIdType.MESH
NT = (((1,), (1,)), ((), ()))
TN = (((0,), (0,)), ((), ()))
GATHER_ORDER = ((0, 1, 2), (1, 2, 0), (2, 0, 1), (0, 1, 2))
SCATTER_ORDER = ((0, 1, 2), (1, 2, 0), (2, 0, 1))
F32 = jnp.float32
BF16 = jnp.bfloat16


def place(n):
    batch, label = lax.axis_index("batch"), lax.axis_index("label")
    core = lax.rem(batch, 2)
    x = lax.rem(lax.div(label, n), n // 2) * 2 + lax.div(batch, 2)
    y = lax.rem(label, n)
    z = lax.div(label, n * (n // 2))
    return (x, y, z), core


def device(n, xyz, core):
    x, y, z = xyz
    return (
        lax.rem(x, 2) * 2 + core,
        z * (n * (n // 2)) + lax.div(x, 2) * n + y,
    )


def kernel(
    n, enc_ref, ids_ref, w_ref, out_ref, grad_ref,
    rows, ids, w_wide, w_low, mask, delta, part, from_core, recv1, sum2, recv2, sum3, recv3, pad, grad,
    w_sem, grad_sem, g_sent_all, g_sent_half, id_sent, g_recv, c_sent, c_recv, x_sent, x_recv, s_sent, s_recv,
):
    me, core = place(n)
    other = 1 - core
    labels = w_ref.shape[0]
    batch, label = lax.axis_index("batch"), lax.axis_index("label")
    offset = (batch * lax.axis_size("label") + label) * labels
    sibling = device(n, me, other)

    def shifted(axis, by):
        return tuple(lax.rem(me[a] + by, n) if a == axis else me[a] for a in range(3))

    w_copy = pltpu.make_async_copy(w_ref, w_wide, w_sem)
    w_copy.start()

    barrier = pltpu.get_barrier_semaphore()
    for axis in range(3):
        for by in range(1, n):
            pl.semaphore_signal(
                barrier, inc=1, device_id=device(n, shifted(axis, by), core), device_id_type=MESH
            )
    pl.semaphore_signal(barrier, inc=1, device_id=sibling, device_id_type=MESH)

    for j in range(3):
        rows[(j, core) + me] = enc_ref[:, j * 256 : (j + 1) * 256]
    pad[:, 0:32] = ids_ref[...]
    lane8 = lax.broadcasted_iota(jnp.int32, (8, 128), 1)
    turned = jnp.concatenate([pad[...]] * 4, axis=0).T
    packed = turned[0:8]
    for q in range(1, 4):
        packed = jnp.where(lax.shift_right_logical(lane8, 5) == q, turned[8 * q : 8 * q + 8], packed)
    ids[(core,) + me] = packed

    pl.semaphore_wait(barrier, 3 * (n - 1) + 1)

    def half(h):
        return slice(16 * h, 16 * h + 16)

    def gathered(j, index):
        return rows.at[(j, core) + index] if j < 3 else ids.at[(core,) + index]

    def remote(src, dst, send_sem, recv_sem, to):
        return pltpu.make_async_remote_copy(
            src_ref=src, dst_ref=dst, send_sem=send_sem, recv_sem=recv_sem,
            device_id=to, device_id_type=MESH,
        )

    def wait_for(ref, sem):
        pltpu.make_async_copy(ref, ref, sem).wait()

    def block_of(j, index, h):
        return gathered(j, index + (half(h),) if j < 3 else index)

    def g_sent(j, step):
        return (id_sent if j == 3 else g_sent_all).at[step]

    def g_copy(j, step, by, h=0, sem=None):
        order = GATHER_ORDER[j]
        index = tuple(slice(None) if a in order[:step] else me[a] for a in range(3))
        ref = block_of(j, index, h)
        to = device(n, shifted(order[step], by), core)
        return remote(ref, ref, g_sent(j, step), g_recv.at[j, h, step if sem is None else sem], to)

    def g_wait(j, step, h=0):
        order = GATHER_ORDER[j]
        index = tuple(
            slice(None) if a in order[:step] else slice(0, n - 1) if a == order[step] else 0 for a in range(3)
        )
        wait_for(block_of(j, index, h), g_recv.at[j, h, step])

    def g_start(j, step, h=0):
        if step > 0:
            g_wait(j, step - 1, h)
        if step == 2:
            c_copy(j, 0, h).start()
        if step == 2 and j < 3 and n == 4:
            g_copy(j, 2, 1, h, 2).start()
            g_copy(j, 2, 3, h, 3).start()
        else:
            for by in range(1, n):
                g_copy(j, step, by, h).start()

    def plane(j, by, h, at=slice(None)):
        first, _, last = GATHER_ORDER[j]
        to = lax.rem(me[last] + n - by, n)
        return block_of(j, tuple(to if a == last else at if a == first else slice(None) for a in range(3)), h)

    def c_copy(j, by, h=0):
        ref = plane(j, by, h)
        return remote(ref, ref, c_sent.at[j // 3], c_recv.at[j, h], sibling)

    def hand_on(h):
        if n == 4:
            for by, at in ((1, slice(0, n // 2)), (3, slice(n // 2, n))):
                for j in thirds:
                    wait_for(plane(j, by, h), g_recv.at[j, h, 2 if by == 1 else 3])
                    ref = plane(j, by, h, at)
                    last = GATHER_ORDER[j][2]
                    remote(ref, ref, g_sent_half, g_recv.at[j, h, 4], device(n, shifted(last, by), core)).start()
                    c_copy(j, by, h).start()

    def pass_on(h):
        for j in thirds:
            if n == 4:
                wait_for(plane(j, 2, h), g_recv.at[j, h, 4])
                c_copy(j, 2, h).start()
            else:
                g_wait(j, 2, h)
                for by in range(1, n):
                    c_copy(j, by, h).start()

    def pass_on_ids():
        g_wait(3, 2)
        for by in range(1, n):
            c_copy(3, by).start()

    def await_core(js, h=0):
        for j in js:
            wait_for(block_of(j, (slice(None),) * 3, h), c_recv.at[j, h])

    thirds = (0, 1, 2)
    for j, step, h in (
        (3, 0, 0), (0, 0, 0), (1, 0, 0), (2, 0, 0),
        (3, 1, 0), (0, 1, 0), (1, 1, 0), (2, 1, 0),
        (3, 2, 0), (0, 0, 1), (1, 0, 1), (2, 0, 1),
        (0, 2, 0), (1, 2, 0), (2, 2, 0),
    ):
        g_start(j, step, h)

    w_copy.wait()

    def narrow(i, _):
        at = pl.ds(pl.multiple_of(i * 128, 128), 128)
        for j in range(3):
            w_low[j, at, :] = w_wide[at, j * 256 : (j + 1) * 256].astype(BF16)
        return 0

    lax.fori_loop(0, labels // 128, narrow, 0)

    sub8 = lax.broadcasted_iota(jnp.int32, (8, 128), 0)
    lane_all = lax.broadcasted_iota(jnp.int32, (128, 128), 1)

    def mask_block(cx, _):
        four = ids[lax.div(cx, n), lax.rem(cx, n)].reshape(n * n, 8, 128)
        for g in range(n * n // 4):
            total = [None] * 4
            for q in range(4):
                local = four[4 * g + q] - offset
                valid = (local >= 0) & (local < labels)
                word = jnp.where(valid, local & 31, -1)
                bit = jnp.left_shift(jnp.int32(1), lax.shift_right_arithmetic(local, 5) & 31)
                held = [None] * 4
                for r in range(8):
                    word_r = jnp.broadcast_to(word[r : r + 1], (8, 128))
                    bit_r = jnp.broadcast_to(bit[r : r + 1], (8, 128))
                    for v in range(4):
                        hit = jnp.where(word_r == sub8 + 8 * v, bit_r, 0)
                        held[v] = hit if held[v] is None else held[v] | hit
                for v in range(4):
                    a = held[v] | pltpu.roll(held[v], 32, 1)
                    a = a | pltpu.roll(a, 64, 1)
                    total[v] = a if q == 0 else jnp.where(lax.shift_right_logical(lane8, 5) == q, a, total[v])
            bits = jnp.concatenate(total * 4, axis=0).T
            bits = lax.shift_right_logical(bits, lax.shift_right_logical(lane_all, 5))
            mask[cx, 4 * g : 4 * g + 4] = bits.reshape(4, 32, 128)
        return 0

    def make_mask(c):
        lax.fori_loop(c * n, c * n + n, mask_block, 0)

    tile = n * n * 16

    def forward(h, c):
        def one(x, _):
            logits = None
            for j in range(3):
                e = rows[j, c, x, :, :, half(h), :].reshape(tile, 256)
                term = lax.dot_general(e, w_low[j], NT, preferred_element_type=F32)
                logits = term if logits is None else logits + term
            bits = mask[c * n + x, :, half(h), :].reshape(tile, 128)
            for t in range(labels // 128):
                sign = jnp.where((bits & (1 << (4 * t))) != 0, -1.0, 1.0)
                at = slice(128 * t, 128 * t + 128)
                d = (jnp.tanh(0.5 * logits[:, at]) + sign).astype(BF16)
                delta[h, c, x, :, :, :, at] = d.reshape(n, n, 16, 128)
            return 0

        lax.fori_loop(0, n, one, 0, unroll=True)

    def encoder_part(h, c, j):
        r = jnp.dot(delta[h, c].reshape(n * tile, labels), w_low[j], preferred_element_type=F32)
        part[j, h, c] = (0.5 * r).astype(BF16).reshape(n, n, n, 16, 256)

    def encoder_quarter(h, j, place):
        at = tuple(place if a == j else slice(None) for a in range(3))
        d = delta[(h, core) + at].reshape(tile, labels)
        r = 0.5 * jnp.dot(d, w_low[j], preferred_element_type=F32)
        r = r + from_core[(j, h) + at].reshape(tile, 256).astype(F32)
        part[(j, h, core) + at] = r.astype(BF16).reshape(n, n, 16, 256)

    def for_sibling(h):
        encoder_part(h, other, 0)
        encoder_part(h, other, 1)
        x_copy(0, h).start()
        x_copy(1, h).start()
        encoder_part(h, other, 2)
        x_copy(2, h).start()

    def for_self(h):
        for j in thirds:
            wait_for(from_core.at[j, h], x_recv.at[j, h])
        far = (2, 1, 3, 0) if n == 4 else tuple(range(n - 1, -1, -1))
        for some in (far[: n // 2], far[n // 2 :]):
            for by in some:
                for j in thirds:
                    encoder_quarter(h, j, lax.rem(me[j] + by, n))
            for by in some:
                for j in thirds:
                    if by > 0:
                        s_copy(j, h, 0, by).start()

    def x_copy(j, h):
        return remote(part.at[j, h, other], from_core.at[j, h], x_sent, x_recv.at[j, h], sibling)

    def s_copy(j, h, step, by):
        order = SCATTER_ORDER[j]
        left = [a for a in range(3) if a not in order[:step]]
        to = shifted(order[step], by)
        index = tuple(to[a] if a == order[step] else slice(None) for a in left)
        src = (part.at[(j, h, core) + index], sum2.at[(j, h) + index], sum3.at[(j, h) + index])[step]
        dst = (recv1, recv2, recv3)[step].at[j, h, by - 1]
        return remote(src, dst, s_sent.at[step], s_recv.at[step, j, h], device(n, to, core))

    def own(j, h, step):
        order = SCATTER_ORDER[j]
        left = [a for a in range(3) if a not in order[:step]]
        index = tuple(me[a] if a == order[step] else slice(None) for a in left)
        ref = (part, sum2, sum3)[step]
        return ref[((j, h, core) if step == 0 else (j, h)) + index].astype(F32)

    def send(j, h, step):
        for by in range(1, n):
            s_copy(j, h, step, by).start()

    def reduce(h, step):
        for j in range(3):
            wait_for((recv1, recv2, recv3)[step].at[j, h], s_recv.at[step, j, h])
            total = own(j, h, step)
            for by in range(1, n):
                total = total + (recv1, recv2, recv3)[step][j, h, by - 1].astype(F32)
            if step == 2:
                out_ref[half(h), j * 256 : (j + 1) * 256] = total.astype(BF16)
            else:
                (sum2, sum3)[step][j, h] = total.astype(BF16)
                send(j, h, step + 1)

    def grad_copy(t):
        at = slice(t * (labels // 4), (t + 1) * (labels // 4))
        return pltpu.make_async_copy(grad.at[at], grad_ref.at[at], grad_sem)

    def grad_part(t):
        size = labels // 4
        at = slice(t * size, (t + 1) * size)
        total = [None] * 3
        for h in range(2):
            for c in range(2):
                d = delta[h, c, :, :, :, :, at].reshape(n * tile, size).T
                for j in thirds:
                    e = rows[j, c, :, :, :, half(h), :].reshape(n * tile, 256)
                    term = jnp.dot(d, e, preferred_element_type=F32)
                    total[j] = term if total[j] is None else total[j] + term
        for j in thirds:
            grad[at, j * 256 : (j + 1) * 256] = 0.5 * total[j]
        grad_copy(t).start()

    pass_on_ids()
    for j in thirds:
        g_start(j, 1, 1)
    make_mask(core)
    hand_on(0)
    await_core((3,))
    make_mask(other)
    pass_on(0)
    for j in thirds:
        g_start(j, 2, 1)
    forward(0, core)
    await_core(thirds, 0)
    forward(0, other)
    hand_on(1)
    for_sibling(0)
    pass_on(1)
    forward(1, core)
    for_self(0)
    await_core(thirds, 1)
    forward(1, other)
    for_sibling(1)
    for_self(1)
    reduce(0, 0)
    grad_part(0)
    grad_part(1)
    grad_part(2)
    reduce(1, 0)
    grad_part(3)
    reduce(0, 1)
    reduce(1, 1)
    reduce(0, 2)
    reduce(1, 2)

    wait_for(grad, grad_sem)
    whole = slice(None)
    for step in range(3):
        per = 2 if step == 2 and n == 4 else n - 1
        index = (slice(0, per),) + ((0, 0), (whole, 0), (whole, whole))[step]
        wait_for(rows.at[(whole, 0) + index], g_sent_all.at[step])
        wait_for(ids.at[(0, slice(0, n - 1)) + index[1:]], id_sent.at[step])
        wait_for((recv1, recv2, recv3)[step], s_sent.at[step])
    if n == 4:
        wait_for(rows.at[:, 0, 0], g_sent_half)
    wait_for(rows.at[:, 0], c_sent.at[0])
    wait_for(ids.at[0], c_sent.at[1])
    wait_for(from_core, x_sent)


def gradients(n, encoded, label_ids, weights):
    labels, width = weights.shape
    vmem = pltpu.VMEM
    dma = pltpu.SemaphoreType.DMA
    return pl.pallas_call(
        functools.partial(kernel, n),
        out_shape=(
            jax.ShapeDtypeStruct(encoded.shape, BF16),
            jax.ShapeDtypeStruct((labels, width), F32),
        ),
        in_specs=[
            pl.BlockSpec(memory_space=pltpu.VMEM),
            pl.BlockSpec(memory_space=pltpu.VMEM),
            pl.BlockSpec(memory_space=pltpu.HBM),
        ],
        out_specs=(
            pl.BlockSpec(memory_space=pltpu.VMEM),
            pl.BlockSpec(memory_space=pl.ANY),
        ),
        scratch_shapes=[
            vmem((3, 2, n, n, n, 32, 256), BF16),
            vmem((2, n, n, n, 8, 128), jnp.int32),
            vmem((labels, width), F32),
            vmem((3, labels, 256), BF16),
            vmem((2 * n, n * n, 32, 128), jnp.int32),
            vmem((2, 2, n, n, n, 16, labels), BF16),
            vmem((3, 2, 2, n, n, n, 16, 256), BF16),
            vmem((3, 2, n, n, n, 16, 256), BF16),
            vmem((3, 2, n - 1, n, n, 16, 256), BF16),
            vmem((3, 2, n, n, 16, 256), BF16),
            vmem((3, 2, n - 1, n, 16, 256), BF16),
            vmem((3, 2, n, 16, 256), BF16),
            vmem((3, 2, n - 1, 16, 256), BF16),
            vmem((32, 128), jnp.int32),
            vmem((labels, width), F32),
            dma,
            dma,
            dma((3,)),
            dma,
            dma((3,)),
            dma((4, 2, 5)),
            dma((2,)),
            dma((4, 2)),
            dma,
            dma((3, 2)),
            dma((3,)),
            dma((3, 3, 2)),
        ],
        compiler_params=pltpu.CompilerParams(
            collective_id=0, has_side_effects=True, vmem_limit_bytes=46 * 2**20
        ),
        name="gradients",
    )(*(pltpu.with_memory_space_constraint(a, pltpu.HBM) for a in (encoded, label_ids, weights)))


def on_device(n, encoded, label_ids, weights, accum):
    encoder_grad, grad = gradients(n, encoded, label_ids, weights)
    new_accum = accum + grad * grad
    new_weights = weights - 0.5 * grad / jnp.sqrt(new_accum)
    return (encoder_grad, new_weights, new_accum)


def solution(mesh):
    n = {4: 2, 32: 4}[mesh.shape["label"]]
    rows = P(("batch", "label"), None)
    return jax.shard_map(
        functools.partial(on_device, n),
        mesh=mesh,
        in_specs=(rows, rows, rows, rows),
        out_specs=(rows, rows, rows),
        check_vma=False,
    )
```

```python
import functools

import jax
import jax.numpy as jnp
from jax import lax
from jax.experimental import pallas as pl
from jax.experimental.pallas import tpu as pltpu
from jax.sharding import PartitionSpec as P

MESH = pl.DeviceIdType.MESH
NT = (((1,), (1,)), ((), ()))
TN = (((0,), (0,)), ((), ()))
GATHER_ORDER = ((0, 1, 2), (1, 2, 0), (2, 0, 1))
ID_ORDER = ((0, 1, 2), (1, 2, 0))
SCATTER_ORDER = ((0, 1, 2), (1, 2, 0), (2, 0, 1))
F32 = jnp.float32
BF16 = jnp.bfloat16


def place(n):
    batch, label = lax.axis_index("batch"), lax.axis_index("label")
    core = lax.rem(batch, 2)
    x = lax.rem(lax.div(label, n), n // 2) * 2 + lax.div(batch, 2)
    y = lax.rem(label, n)
    z = lax.div(label, n * (n // 2))
    return (x, y, z), core


def device(n, xyz, core):
    x, y, z = xyz
    return (
        lax.rem(x, 2) * 2 + core,
        z * (n * (n // 2)) + lax.div(x, 2) * n + y,
    )


def kernel(
    n, enc_ref, ids_ref, w_ref, a_ref, out_ref, new_w_ref, new_a_ref,
    rows, ids, w_wide, w_low, mask, delta, part, from_core, recv1, sum2, recv2, sum3, recv3, pad, a_wide, held,
    w_sem, a_sem, new_w_sem, new_a_sem, g_sent_all, g_sent_half, id_sent, g_recv, c_sent, c_recv, x_sent, x_recv, s_sent, s_recv,
):
    me, core = place(n)
    other = 1 - core
    labels = w_ref.shape[0]
    batch, label = lax.axis_index("batch"), lax.axis_index("label")
    offset = (batch * lax.axis_size("label") + label) * labels
    sibling = device(n, me, other)

    far = (2, 1, 3) if n == 4 else tuple(range(n - 1, 0, -1))

    def shifted(axis, by):
        return tuple(lax.rem(me[a] + by, n) if a == axis else me[a] for a in range(3))

    w_copy = pltpu.make_async_copy(w_ref, w_wide, w_sem)
    w_copy.start()
    pltpu.make_async_copy(a_ref, a_wide, a_sem).start()

    barrier = pltpu.get_barrier_semaphore()
    for axis in range(3):
        for by in range(1, n):
            pl.semaphore_signal(
                barrier, inc=1, device_id=device(n, shifted(axis, by), core), device_id_type=MESH
            )
    pl.semaphore_signal(barrier, inc=1, device_id=sibling, device_id_type=MESH)

    for j in range(3):
        rows[(j, core) + me] = enc_ref[:, j * 256 : (j + 1) * 256]
    pad[:, 0:32] = ids_ref[...]
    lane8 = lax.broadcasted_iota(jnp.int32, (8, 128), 1)
    turned = jnp.concatenate([pad[...]] * 4, axis=0).T
    packed = turned[0:8]
    for q in range(1, 4):
        packed = jnp.where(lax.shift_right_logical(lane8, 5) == q, turned[8 * q : 8 * q + 8], packed)
    ids[(core,) + me] = packed

    pl.semaphore_wait(barrier, 3 * (n - 1) + 1)

    def half(h):
        return slice(16 * h, 16 * h + 16)

    def gathered(j, index):
        return rows.at[(j, core) + index] if j < 3 else ids.at[(core,) + index]

    def remote(src, dst, send_sem, recv_sem, to):
        return pltpu.make_async_remote_copy(
            src_ref=src, dst_ref=dst, send_sem=send_sem, recv_sem=recv_sem,
            device_id=to, device_id_type=MESH,
        )

    def wait_for(ref, sem):
        pltpu.make_async_copy(ref, ref, sem).wait()

    def block_of(j, index, h):
        return gathered(j, index + (half(h),) if j < 3 else index)

    def g_copy(j, step, by, h=0, sem=None, order=None):
        order = order or GATHER_ORDER[j]
        index = tuple(slice(None) if a in order[:step] else me[a] for a in range(3))
        ref = block_of(j, index, h)
        to = device(n, shifted(order[step], by), core)
        sent = (id_sent if j == 3 else g_sent_all).at[step]
        return remote(ref, ref, sent, g_recv.at[j, h, step if sem is None else sem], to)

    def g_wait(j, step, h=0):
        order = GATHER_ORDER[j % 3]
        index = tuple(
            slice(None) if a in order[:step] else slice(0, n - 1) if a == order[step] else 0 for a in range(3)
        )
        wait_for(block_of(j, index, h), g_recv.at[j, h, step])

    def by_core(act):
        for c in range(2):
            pl.when(core == c)(functools.partial(act, ID_ORDER[c]))

    def id_start(step):
        if step > 0:
            g_wait(3, step - 1)

        def act(order):
            if step == 2:
                c_copy(3, 0, order=order).start()
            for by in far:
                g_copy(3, step, by, order=order).start()

        by_core(act)

    def g_start(j, step, h=0):
        if j == 3:
            return id_start(step)
        if step > 0:
            g_wait(j, step - 1, h)
        if step == 2:
            c_copy(j, 0, h).start()
        if step == 2 and n == 4:
            g_copy(j, 2, 1, h, 2).start()
            g_copy(j, 2, 3, h, 3).start()
        else:
            for by in far:
                g_copy(j, step, by, h).start()

    def plane(j, by, h, at=slice(None), order=None):
        first, _, last = order or GATHER_ORDER[j]
        to = lax.rem(me[last] + n - by, n)
        return block_of(j, tuple(to if a == last else at if a == first else slice(None) for a in range(3)), h)

    def c_copy(j, by, h=0, order=None):
        ref = plane(j, by, h, order=order)
        return remote(ref, ref, c_sent.at[j // 3], c_recv.at[j, h], sibling)

    def hand_on(h):
        if n == 4:
            for by, at in ((1, slice(0, n // 2)), (3, slice(n // 2, n))):
                for j in thirds:
                    wait_for(plane(j, by, h), g_recv.at[j, h, 2 if by == 1 else 3])
                    ref = plane(j, by, h, at)
                    last = GATHER_ORDER[j][2]
                    remote(ref, ref, g_sent_half, g_recv.at[j, h, 4], device(n, shifted(last, by), core)).start()
                    c_copy(j, by, h).start()

    def pass_on(h):
        for j in thirds:
            if n == 4:
                wait_for(plane(j, 2, h), g_recv.at[j, h, 4])
                c_copy(j, 2, h).start()
            else:
                g_wait(j, 2, h)
                for by in range(1, n):
                    c_copy(j, by, h).start()

    def pass_on_ids():
        g_wait(3, 2)

        def act(order):
            for by in range(1, n):
                c_copy(3, by, order=order).start()

        by_core(act)

    def await_core(js, h=0):
        for j in js:
            wait_for(block_of(j, (slice(None),) * 3, h), c_recv.at[j, h])

    thirds = (0, 1, 2)
    for j, step, h in (
        (3, 0, 0), (0, 0, 0), (1, 0, 0), (2, 0, 0),
        (3, 1, 0), (0, 1, 0), (1, 1, 0), (2, 1, 0),
        (3, 2, 0), (0, 0, 1), (1, 0, 1), (2, 0, 1),
        (0, 2, 0), (1, 2, 0), (2, 2, 0),
    ):
        g_start(j, step, h)

    w_copy.wait()

    def narrow(i, _):
        at = pl.ds(pl.multiple_of(i * 128, 128), 128)
        for j in range(3):
            w_low[j, at, :] = w_wide[at, j * 256 : (j + 1) * 256].astype(BF16)
        return 0

    lax.fori_loop(0, labels // 128, narrow, 0)

    sub8 = lax.broadcasted_iota(jnp.int32, (8, 128), 0)
    lane_all = lax.broadcasted_iota(jnp.int32, (128, 128), 1)

    def mask_block(cx, _):
        four = ids[lax.div(cx, n), lax.rem(cx, n)].reshape(n * n, 8, 128)
        for g in range(n * n // 4):
            total = [None] * 4
            for q in range(4):
                local = four[4 * g + q] - offset
                valid = (local >= 0) & (local < labels)
                word = jnp.where(valid, local & 31, -1)
                bit = jnp.left_shift(jnp.int32(1), lax.shift_right_arithmetic(local, 5) & 31)
                held = [None] * 4
                for r in range(8):
                    word_r = jnp.broadcast_to(word[r : r + 1], (8, 128))
                    bit_r = jnp.broadcast_to(bit[r : r + 1], (8, 128))
                    for v in range(4):
                        hit = jnp.where(word_r == sub8 + 8 * v, bit_r, 0)
                        held[v] = hit if held[v] is None else held[v] | hit
                for v in range(4):
                    a = held[v] | pltpu.roll(held[v], 32, 1)
                    a = a | pltpu.roll(a, 64, 1)
                    total[v] = a if q == 0 else jnp.where(lax.shift_right_logical(lane8, 5) == q, a, total[v])
            bits = jnp.concatenate(total * 4, axis=0).T
            bits = lax.shift_right_logical(bits, lax.shift_right_logical(lane_all, 5))
            mask[cx, 4 * g : 4 * g + 4] = bits.reshape(4, 32, 128)
        return 0

    def make_mask(c, first, last):
        lax.fori_loop(c * n + first, c * n + last, mask_block, 0)

    tile = n * n * 16

    def forward(h, c):
        def one(x, _):
            logits = None
            for j in range(3):
                e = rows[j, c, x, :, :, half(h), :].reshape(tile, 256)
                term = lax.dot_general(e, w_low[j], NT, preferred_element_type=F32)
                logits = term if logits is None else logits + term
            bits = mask[c * n + x, :, half(h), :].reshape(tile, 128)
            for t in range(labels // 128):
                sign = jnp.where((bits & (1 << (4 * t))) != 0, -1.0, 1.0)
                at = slice(128 * t, 128 * t + 128)
                d = (jnp.tanh(0.5 * logits[:, at]) + sign).astype(BF16)
                delta[h, c, x, :, :, :, at] = d.reshape(n, n, 16, 128)
            return 0

        lax.fori_loop(0, n, one, 0, unroll=True)

    def encoder_part(h, c, j):
        r = jnp.dot(delta[h, c].reshape(n * tile, labels), w_low[j], preferred_element_type=F32)
        part[j, h, c] = (0.5 * r).astype(BF16).reshape(n, n, n, 16, 256)

    def quarter(j, by):
        place = lax.rem(me[j] + by, n)
        return tuple(place if a == j else slice(None) for a in range(3))

    def quarter_sums(h, j, by):
        d = delta[(h, core) + quarter(j, by)].reshape(tile, labels)
        return 0.5 * jnp.dot(d, w_low[j], preferred_element_type=F32)

    def add_sibling(h, j, by, sums):
        at = quarter(j, by)
        r = sums + from_core[(j, h) + at].reshape(tile, 256).astype(F32)
        part[(j, h, core) + at] = r.astype(BF16).reshape(n, n, 16, 256)

    def for_sibling(h):
        encoder_part(h, other, 0)
        encoder_part(h, other, 1)
        x_copy(0, h).start()
        x_copy(1, h).start()
        encoder_part(h, other, 2)
        x_copy(2, h).start()

    def for_self(h, early):
        order = far + (0,)
        first = [(j, by) for by in order[: n // 2] for j in thirds]
        rest = [(j, by) for by in order[n // 2 :] for j in thirds]
        if early:
            for i, (j, by) in enumerate(first):
                held[i] = quarter_sums(h, j, by)
        for j in thirds:
            wait_for(from_core.at[j, h], x_recv.at[j, h])
        for some in (first, rest):
            for i, (j, by) in enumerate(some):
                add_sibling(h, j, by, held[i] if early and some is first else quarter_sums(h, j, by))
            for j, by in some:
                if by > 0:
                    s_copy(j, h, 0, by).start()

    def x_copy(j, h):
        return remote(part.at[j, h, other], from_core.at[j, h], x_sent, x_recv.at[j, h], sibling)

    def s_copy(j, h, step, by):
        order = SCATTER_ORDER[j]
        left = [a for a in range(3) if a not in order[:step]]
        to = shifted(order[step], by)
        index = tuple(to[a] if a == order[step] else slice(None) for a in left)
        src = (part.at[(j, h, core) + index], sum2.at[(j, h) + index], sum3.at[(j, h) + index])[step]
        dst = (recv1, recv2, recv3)[step].at[j, h, by - 1]
        return remote(src, dst, s_sent.at[step], s_recv.at[step, j, h], device(n, to, core))

    def own(j, h, step):
        order = SCATTER_ORDER[j]
        left = [a for a in range(3) if a not in order[:step]]
        index = tuple(me[a] if a == order[step] else slice(None) for a in left)
        ref = (part, sum2, sum3)[step]
        return ref[((j, h, core) if step == 0 else (j, h)) + index].astype(F32)

    def send(j, h, step):
        for by in far:
            s_copy(j, h, step, by).start()

    def reduce(h, step):
        for j in range(3):
            wait_for((recv1, recv2, recv3)[step].at[j, h], s_recv.at[step, j, h])
            total = own(j, h, step)
            for by in range(1, n):
                total = total + (recv1, recv2, recv3)[step][j, h, by - 1].astype(F32)
            if step == 2:
                out_ref[half(h), j * 256 : (j + 1) * 256] = total.astype(BF16)
            else:
                (sum2, sum3)[step][j, h] = total.astype(BF16)
                send(j, h, step + 1)

    def grad_part(t):
        size = labels // 4
        at = slice(t * size, (t + 1) * size)
        total = [None] * 3
        for h in range(2):
            for c in range(2):
                d = delta[h, c, :, :, :, :, at].reshape(n * tile, size).T
                for j in thirds:
                    e = rows[j, c, :, :, :, half(h), :].reshape(n * tile, 256)
                    term = jnp.dot(d, e, preferred_element_type=F32)
                    total[j] = term if total[j] is None else total[j] + term
        for j in thirds:
            columns = slice(j * 256, (j + 1) * 256)
            grad = 0.5 * total[j]
            new = a_wide[at, columns] + grad * grad
            a_wide[at, columns] = new
            w_wide[at, columns] = w_wide[at, columns] - 0.5 * grad * lax.rsqrt(new)
        pltpu.make_async_copy(a_wide.at[at], new_a_ref.at[at], new_a_sem).start()
        pltpu.make_async_copy(w_wide.at[at], new_w_ref.at[at], new_w_sem).start()

    pass_on_ids()
    for j in thirds:
        g_start(j, 1, 1)
    make_mask(core, 0, n)
    hand_on(0)
    await_core((3,))
    make_mask(other, 0, n // 2)
    for j in thirds:
        g_start(j, 2, 1)
    make_mask(other, n // 2, n)
    pass_on(0)
    forward(0, core)
    hand_on(1)
    await_core(thirds, 0)
    forward(0, other)
    for_sibling(0)
    pass_on(1)
    forward(1, core)
    for_self(0, False)
    await_core(thirds, 1)
    forward(1, other)
    for_sibling(1)
    for_self(1, True)
    reduce(0, 0)
    wait_for(a_wide, a_sem)
    grad_part(0)
    grad_part(1)
    grad_part(2)
    reduce(1, 0)
    grad_part(3)
    reduce(0, 1)
    reduce(1, 1)
    reduce(0, 2)
    reduce(1, 2)

    wait_for(a_wide, new_a_sem)
    wait_for(w_wide, new_w_sem)
    whole = slice(None)
    for step in range(3):
        per = 2 if step == 2 and n == 4 else n - 1
        index = (slice(0, per),) + ((0, 0), (whole, 0), (whole, whole))[step]
        wait_for(rows.at[(whole, 0) + index], g_sent_all.at[step])
        wait_for(ids.at[(0, slice(0, n - 1)) + index[1:]], id_sent.at[step])
        wait_for((recv1, recv2, recv3)[step], s_sent.at[step])
    if n == 4:
        wait_for(rows.at[:, 0, 0], g_sent_half)
    wait_for(rows.at[:, 0], c_sent.at[0])
    wait_for(ids.at[0], c_sent.at[1])
    wait_for(from_core, x_sent)


def step(n, encoded, label_ids, weights, accum):
    labels, width = weights.shape
    vmem = pltpu.VMEM
    dma = pltpu.SemaphoreType.DMA
    results = pl.pallas_call(
        functools.partial(kernel, n),
        out_shape=(
            jax.ShapeDtypeStruct(encoded.shape, BF16),
            jax.ShapeDtypeStruct((labels, width), F32),
            jax.ShapeDtypeStruct((labels, width), F32),
        ),
        in_specs=[
            pl.BlockSpec(memory_space=pltpu.VMEM),
            pl.BlockSpec(memory_space=pltpu.VMEM),
            pl.BlockSpec(memory_space=pltpu.HBM),
            pl.BlockSpec(memory_space=pltpu.HBM),
        ],
        out_specs=(
            pl.BlockSpec(memory_space=pltpu.VMEM),
            pl.BlockSpec(memory_space=pl.ANY),
            pl.BlockSpec(memory_space=pl.ANY),
        ),
        scratch_shapes=[
            vmem((3, 2, n, n, n, 32, 256), BF16),
            vmem((2, n, n, n, 8, 128), jnp.int32),
            vmem((labels, width), F32),
            vmem((3, labels, 256), BF16),
            vmem((2 * n, n * n, 32, 128), jnp.int32),
            vmem((2, 2, n, n, n, 16, labels), BF16),
            vmem((3, 2, 2, n, n, n, 16, 256), BF16),
            vmem((3, 2, n, n, n, 16, 256), BF16),
            vmem((3, 2, n - 1, n, n, 16, 256), BF16),
            vmem((3, 2, n, n, 16, 256), BF16),
            vmem((3, 2, n - 1, n, 16, 256), BF16),
            vmem((3, 2, n, 16, 256), BF16),
            vmem((3, 2, n - 1, 16, 256), BF16),
            vmem((32, 128), jnp.int32),
            vmem((labels, width), F32),
            vmem((3 * (n // 2), n * n * 16, 256), F32),
            dma,
            dma,
            dma,
            dma,
            dma((3,)),
            dma,
            dma((3,)),
            dma((4, 2, 5)),
            dma((2,)),
            dma((4, 2)),
            dma,
            dma((3, 2)),
            dma((3,)),
            dma((3, 3, 2)),
        ],
        compiler_params=pltpu.CompilerParams(
            collective_id=0, has_side_effects=True, vmem_limit_bytes=46 * 2**20
        ),
        name="gradients",
    )(*(pltpu.with_memory_space_constraint(a, pltpu.HBM) for a in (encoded, label_ids, weights, accum)))
    return store(*results)


def store_kernel(pieces, *refs):
    count = len(pieces)
    sources, targets, sems = refs[:count], refs[count : 2 * count], refs[2 * count]
    copies = []
    for source, target, parts in zip(sources, targets, pieces):
        size = source.shape[0] // parts
        for p in range(parts):
            at = pl.ds(p * size, size)
            copies.append(pltpu.make_async_copy(source.at[at], target.at[at], sems.at[len(copies)]))
    for copy in copies:
        copy.start()
    for copy in copies:
        copy.wait()


def store(*arrays):
    pieces = (1, 4, 4)
    return pl.pallas_call(
        functools.partial(store_kernel, pieces),
        out_shape=tuple(jax.ShapeDtypeStruct(a.shape, a.dtype) for a in arrays),
        in_specs=[pl.BlockSpec(memory_space=pltpu.VMEM)] * len(arrays),
        out_specs=(pl.BlockSpec(memory_space=pltpu.HBM),) * len(arrays),
        scratch_shapes=[pltpu.SemaphoreType.DMA((sum(pieces),))],
        compiler_params=pltpu.CompilerParams(vmem_limit_bytes=16 * 2**20),
        name="store",
    )(*arrays)


def solution(mesh):
    n = {4: 2, 32: 4}[mesh.shape["label"]]
    rows = P(("batch", "label"), None)
    return jax.shard_map(
        functools.partial(step, n),
        mesh=mesh,
        in_specs=(rows, rows, rows, rows),
        out_specs=(rows, rows, rows),
        check_vma=False,
    )
```

```python
import functools

import jax
import jax.numpy as jnp
from jax import lax
from jax.experimental import pallas as pl
from jax.experimental.pallas import tpu as pltpu
from jax.sharding import PartitionSpec as P

MESH = pl.DeviceIdType.MESH
NT = (((1,), (1,)), ((), ()))
TN = (((0,), (0,)), ((), ()))
GATHER_ORDER = ((0, 1, 2), (1, 2, 0), (2, 0, 1))
ID_ORDER = ((0, 1, 2), (1, 2, 0))
SCATTER_ORDER = ((0, 1, 2), (1, 2, 0), (2, 0, 1))
F32 = jnp.float32
BF16 = jnp.bfloat16


def place(n):
    batch, label = lax.axis_index("batch"), lax.axis_index("label")
    core = lax.rem(batch, 2)
    x = lax.rem(lax.div(label, n), n // 2) * 2 + lax.div(batch, 2)
    y = lax.rem(label, n)
    z = lax.div(label, n * (n // 2))
    return (x, y, z), core


def device(n, xyz, core):
    x, y, z = xyz
    return (
        lax.rem(x, 2) * 2 + core,
        z * (n * (n // 2)) + lax.div(x, 2) * n + y,
    )


def kernel(
    n, enc_ref, ids_ref, w_ref, a_ref, out_ref, new_w_ref, new_a_ref,
    rows, ids, w_wide, w_low, mask, delta, part, from_core, recv1, sum2, recv2, sum3, recv3, pad, a_wide, held,
    w_sem, a_sem, new_w_sem, new_a_sem, g_sent_all, g_sent_half, id_sent, g_recv, c_sent, c_recv, x_sent, x_recv, s_sent, s_recv, s_relay,
):
    me, core = place(n)
    other = 1 - core
    labels = w_ref.shape[0]
    batch, label = lax.axis_index("batch"), lax.axis_index("label")
    offset = (batch * lax.axis_size("label") + label) * labels
    sibling = device(n, me, other)

    far = (2, 1, 3) if n == 4 else tuple(range(n - 1, 0, -1))

    def shifted(axis, by):
        return tuple(lax.rem(me[a] + by, n) if a == axis else me[a] for a in range(3))

    w_copy = pltpu.make_async_copy(w_ref, w_wide, w_sem)
    w_copy.start()
    pltpu.make_async_copy(a_ref, a_wide, a_sem).start()

    barrier = pltpu.get_barrier_semaphore()
    for axis in range(3):
        for by in range(1, n):
            pl.semaphore_signal(
                barrier, inc=1, device_id=device(n, shifted(axis, by), core), device_id_type=MESH
            )
    pl.semaphore_signal(barrier, inc=1, device_id=sibling, device_id_type=MESH)

    for j in range(3):
        rows[(j, core) + me] = enc_ref[:, j * 256 : (j + 1) * 256]
    pad[:, 0:32] = ids_ref[...]
    lane8 = lax.broadcasted_iota(jnp.int32, (8, 128), 1)
    turned = jnp.concatenate([pad[...]] * 4, axis=0).T
    packed = turned[0:8]
    for q in range(1, 4):
        packed = jnp.where(lax.shift_right_logical(lane8, 5) == q, turned[8 * q : 8 * q + 8], packed)
    ids[(core,) + me] = packed

    pl.semaphore_wait(barrier, 3 * (n - 1) + 1)

    def half(h):
        return slice(16 * h, 16 * h + 16)

    def gathered(j, index):
        return rows.at[(j, core) + index] if j < 3 else ids.at[(core,) + index]

    def remote(src, dst, send_sem, recv_sem, to):
        return pltpu.make_async_remote_copy(
            src_ref=src, dst_ref=dst, send_sem=send_sem, recv_sem=recv_sem,
            device_id=to, device_id_type=MESH,
        )

    def wait_for(ref, sem):
        pltpu.make_async_copy(ref, ref, sem).wait()

    def block_of(j, index, h):
        return gathered(j, index + (half(h),) if j < 3 else index)

    def g_copy(j, step, by, h=0, sem=None, order=None):
        order = order or GATHER_ORDER[j]
        index = tuple(slice(None) if a in order[:step] else me[a] for a in range(3))
        ref = block_of(j, index, h)
        to = device(n, shifted(order[step], by), core)
        sent = (id_sent if j == 3 else g_sent_all).at[step]
        return remote(ref, ref, sent, g_recv.at[j, h, step if sem is None else sem], to)

    def g_wait(j, step, h=0):
        order = GATHER_ORDER[j % 3]
        index = tuple(
            slice(None) if a in order[:step] else slice(0, n - 1) if a == order[step] else 0 for a in range(3)
        )
        wait_for(block_of(j, index, h), g_recv.at[j, h, step])

    def by_core(act):
        for c in range(2):
            pl.when(core == c)(functools.partial(act, ID_ORDER[c]))

    def id_start(step):
        if step > 0:
            g_wait(3, step - 1)

        def act(order):
            if step == 2:
                c_copy(3, 0, order=order).start()
            for by in far:
                g_copy(3, step, by, order=order).start()

        by_core(act)

    def g_start(j, step, h=0):
        if j == 3:
            return id_start(step)
        if step > 0:
            g_wait(j, step - 1, h)
        if step == 2:
            c_copy(j, 0, h).start()
        if step == 2 and n == 4:
            g_copy(j, 2, 1, h, 2).start()
            g_copy(j, 2, 3, h, 3).start()
        else:
            for by in far:
                g_copy(j, step, by, h).start()

    def plane(j, by, h, at=slice(None), order=None):
        first, _, last = order or GATHER_ORDER[j]
        to = lax.rem(me[last] + n - by, n)
        return block_of(j, tuple(to if a == last else at if a == first else slice(None) for a in range(3)), h)

    def c_copy(j, by, h=0, order=None):
        ref = plane(j, by, h, order=order)
        return remote(ref, ref, c_sent.at[j // 3], c_recv.at[j, h], sibling)

    def hand_on(h):
        if n == 4:
            for by, at in ((1, slice(0, n // 2)), (3, slice(n // 2, n))):
                for j in thirds:
                    wait_for(plane(j, by, h), g_recv.at[j, h, 2 if by == 1 else 3])
                    ref = plane(j, by, h, at)
                    last = GATHER_ORDER[j][2]
                    remote(ref, ref, g_sent_half, g_recv.at[j, h, 4], device(n, shifted(last, by), core)).start()
                    c_copy(j, by, h).start()

    def pass_on(h):
        for j in thirds:
            if n == 4:
                wait_for(plane(j, 2, h), g_recv.at[j, h, 4])
                c_copy(j, 2, h).start()
            else:
                g_wait(j, 2, h)
                for by in range(1, n):
                    c_copy(j, by, h).start()

    def pass_on_ids():
        g_wait(3, 2)

        def act(order):
            for by in range(1, n):
                c_copy(3, by, order=order).start()

        by_core(act)

    def await_core(js, h=0):
        for j in js:
            wait_for(block_of(j, (slice(None),) * 3, h), c_recv.at[j, h])

    thirds = (0, 1, 2)
    for j, step, h in (
        (3, 0, 0), (0, 0, 0), (1, 0, 0), (2, 0, 0),
        (3, 1, 0), (0, 1, 0), (1, 1, 0), (2, 1, 0),
        (3, 2, 0), (0, 0, 1), (1, 0, 1), (2, 0, 1),
        (0, 2, 0), (1, 2, 0), (2, 2, 0),
    ):
        g_start(j, step, h)

    w_copy.wait()

    def narrow(i, _):
        at = pl.ds(pl.multiple_of(i * 128, 128), 128)
        for j in range(3):
            w_low[j, at, :] = w_wide[at, j * 256 : (j + 1) * 256].astype(BF16)
        return 0

    lax.fori_loop(0, labels // 128, narrow, 0)

    sub8 = lax.broadcasted_iota(jnp.int32, (8, 128), 0)
    lane_all = lax.broadcasted_iota(jnp.int32, (128, 128), 1)

    def mask_block(cx, _):
        four = ids[lax.div(cx, n), lax.rem(cx, n)].reshape(n * n, 8, 128)
        for g in range(n * n // 4):
            total = [None] * 4
            for q in range(4):
                local = four[4 * g + q] - offset
                valid = (local >= 0) & (local < labels)
                word = jnp.where(valid, local & 31, -1)
                bit = jnp.left_shift(jnp.int32(1), lax.shift_right_arithmetic(local, 5) & 31)
                held = [None] * 4
                for r in range(8):
                    word_r = jnp.broadcast_to(word[r : r + 1], (8, 128))
                    bit_r = jnp.broadcast_to(bit[r : r + 1], (8, 128))
                    for v in range(4):
                        hit = jnp.where(word_r == sub8 + 8 * v, bit_r, 0)
                        held[v] = hit if held[v] is None else held[v] | hit
                for v in range(4):
                    a = held[v] | pltpu.roll(held[v], 32, 1)
                    a = a | pltpu.roll(a, 64, 1)
                    total[v] = a if q == 0 else jnp.where(lax.shift_right_logical(lane8, 5) == q, a, total[v])
            bits = jnp.concatenate(total * 4, axis=0).T
            bits = lax.shift_right_logical(bits, lax.shift_right_logical(lane_all, 5))
            mask[cx, 4 * g : 4 * g + 4] = bits.reshape(4, 32, 128)
        return 0

    def make_mask(c, first, last):
        lax.fori_loop(c * n + first, c * n + last, mask_block, 0)

    tile = n * n * 16

    def forward(h, c):
        def one(x, _):
            logits = None
            for j in range(3):
                e = rows[j, c, x, :, :, half(h), :].reshape(tile, 256)
                term = lax.dot_general(e, w_low[j], NT, preferred_element_type=F32)
                logits = term if logits is None else logits + term
            bits = mask[c * n + x, :, half(h), :].reshape(tile, 128)
            for t in range(labels // 128):
                sign = jnp.where((bits & (1 << (4 * t))) != 0, -1.0, 1.0)
                at = slice(128 * t, 128 * t + 128)
                d = (jnp.tanh(0.5 * logits[:, at]) + sign).astype(BF16)
                delta[h, c, x, :, :, :, at] = d.reshape(n, n, 16, 128)
            return 0

        lax.fori_loop(0, n, one, 0, unroll=True)

    def encoder_part(h, c, j):
        r = jnp.dot(delta[h, c].reshape(n * tile, labels), w_low[j], preferred_element_type=F32)
        part[j, h, c] = (0.5 * r).astype(BF16).reshape(n, n, n, 16, 256)

    def quarter(j, by):
        place = lax.rem(me[j] + by, n)
        return tuple(place if a == j else slice(None) for a in range(3))

    def quarter_sums(h, j, by):
        d = delta[(h, core) + quarter(j, by)].reshape(tile, labels)
        return 0.5 * jnp.dot(d, w_low[j], preferred_element_type=F32)

    def add_sibling(h, j, by, sums):
        at = quarter(j, by)
        r = sums + from_core[(j, h) + at].reshape(tile, 256).astype(F32)
        part[(j, h, core) + at] = r.astype(BF16).reshape(n, n, 16, 256)

    def for_sibling(h):
        encoder_part(h, other, 0)
        encoder_part(h, other, 1)
        x_copy(0, h).start()
        x_copy(1, h).start()
        encoder_part(h, other, 2)
        x_copy(2, h).start()

    def for_self(h, early):
        order = far + (0,)
        first = [(j, by) for by in order[: n // 2] for j in thirds]
        rest = [(j, by) for by in order[n // 2 :] for j in thirds]
        if early:
            for i, (j, by) in enumerate(first):
                held[i] = quarter_sums(h, j, by)
        for j in thirds:
            wait_for(from_core.at[j, h], x_recv.at[j, h])
        for some in (first, rest):
            for i, (j, by) in enumerate(some):
                add_sibling(h, j, by, held[i] if early and some is first else quarter_sums(h, j, by))
            for j, by in some:
                if by > 0 and early and n == 4:
                    by_halves(j, by)
                elif by > 0:
                    s_copy(j, h, 0, by).start()

    def x_copy(j, h):
        return remote(part.at[j, h, other], from_core.at[j, h], x_sent, x_recv.at[j, h], sibling)

    def s_copy(j, h, step, by):
        order = SCATTER_ORDER[j]
        left = [a for a in range(3) if a not in order[:step]]
        to = shifted(order[step], by)
        index = tuple(to[a] if a == order[step] else slice(None) for a in left)
        src = (part.at[(j, h, core) + index], sum2.at[(j, h) + index], sum3.at[(j, h) + index])[step]
        dst = (recv1, recv2, recv3)[step].at[j, h, by - 1]
        return remote(src, dst, s_sent.at[step], s_recv.at[step, j, h], device(n, to, core))

    def half_block(j, by, upper):
        cut = slice(n // 2, n) if upper else slice(0, n // 2)
        place = lax.rem(me[j] + by, n)
        other_axis = 1 if j == 0 else 0
        index = tuple(place if a == j else cut if a == other_axis else slice(None) for a in range(3))
        return (j, 1, core) + index, cut

    def half_copy(j, by, upper, to, slot, sem):
        at, cut = half_block(j, by, upper)
        return remote(part.at[at], recv1.at[j, 1, slot, cut], s_sent.at[0], sem, device(n, shifted(j, to), core))

    def by_halves(j, by):
        if by == 2:
            half_copy(j, 2, False, 1, 1, s_relay.at[j]).start()
            half_copy(j, 2, True, 3, 1, s_relay.at[j]).start()
        else:
            half_copy(j, by, by == 1, by, by - 1, s_recv.at[0, j, 1]).start()

    def relay():
        if n == 4:
            for j in thirds:
                wait_for(recv1.at[j, 1, 1], s_relay.at[j])
                for by in (1, 3):
                    at, cut = half_block(j, by, by == 3)
                    part[at] = (part[at].astype(F32) + recv1[j, 1, 1, cut].astype(F32)).astype(BF16)
                for by in (1, 3):
                    half_copy(j, by, by == 3, by, by - 1, s_recv.at[0, j, 1]).start()

    def own(j, h, step):
        order = SCATTER_ORDER[j]
        left = [a for a in range(3) if a not in order[:step]]
        index = tuple(me[a] if a == order[step] else slice(None) for a in left)
        ref = (part, sum2, sum3)[step]
        return ref[((j, h, core) if step == 0 else (j, h)) + index].astype(F32)

    def send(j, h, step):
        for by in far:
            s_copy(j, h, step, by).start()

    def reduce(h, step):
        for j in range(3):
            halved = n == 4 and h == 1 and step == 0
            arrived = (recv1, recv2, recv3)[step].at[j, h]
            wait_for(arrived.at[0:2] if halved else arrived, s_recv.at[step, j, h])
            total = own(j, h, step)
            for by in (1, 3) if halved else range(1, n):
                total = total + (recv1, recv2, recv3)[step][j, h, by - 1].astype(F32)
            if step == 2:
                out_ref[half(h), j * 256 : (j + 1) * 256] = total.astype(BF16)
            else:
                (sum2, sum3)[step][j, h] = total.astype(BF16)
                send(j, h, step + 1)

    def grad_part(t):
        size = labels // 4
        at = slice(t * size, (t + 1) * size)
        total = [None] * 3
        for h in range(2):
            for c in range(2):
                d = delta[h, c, :, :, :, :, at].reshape(n * tile, size).T
                for j in thirds:
                    e = rows[j, c, :, :, :, half(h), :].reshape(n * tile, 256)
                    term = jnp.dot(d, e, preferred_element_type=F32)
                    total[j] = term if total[j] is None else total[j] + term
        for j in thirds:
            columns = slice(j * 256, (j + 1) * 256)
            grad = 0.5 * total[j]
            new = a_wide[at, columns] + grad * grad
            a_wide[at, columns] = new
            w_wide[at, columns] = w_wide[at, columns] - 0.5 * grad * lax.rsqrt(new)
        pltpu.make_async_copy(a_wide.at[at], new_a_ref.at[at], new_a_sem).start()
        pltpu.make_async_copy(w_wide.at[at], new_w_ref.at[at], new_w_sem).start()

    pass_on_ids()
    for j in thirds:
        g_start(j, 1, 1)
    make_mask(core, 0, n)
    hand_on(0)
    await_core((3,))
    make_mask(other, 0, n // 2)
    for j in thirds:
        g_start(j, 2, 1)
    make_mask(other, n // 2, n)
    pass_on(0)
    forward(0, core)
    hand_on(1)
    await_core(thirds, 0)
    forward(0, other)
    for_sibling(0)
    pass_on(1)
    forward(1, core)
    for_self(0, False)
    await_core(thirds, 1)
    forward(1, other)
    for_sibling(1)
    for_self(1, True)
    wait_for(a_wide, a_sem)
    grad_part(0)
    relay()
    reduce(0, 0)
    grad_part(1)
    reduce(1, 0)
    grad_part(2)
    reduce(0, 1)
    reduce(1, 1)
    grad_part(3)
    reduce(0, 2)
    reduce(1, 2)

    wait_for(a_wide, new_a_sem)
    wait_for(w_wide, new_w_sem)
    whole = slice(None)
    for step in range(3):
        per = 2 if step == 2 and n == 4 else n - 1
        index = (slice(0, per),) + ((0, 0), (whole, 0), (whole, whole))[step]
        wait_for(rows.at[(whole, 0) + index], g_sent_all.at[step])
        wait_for(ids.at[(0, slice(0, n - 1)) + index[1:]], id_sent.at[step])
        wait_for((recv1, recv2, recv3)[step], s_sent.at[step])
    if n == 4:
        wait_for(rows.at[:, 0, 0], g_sent_half)
    wait_for(rows.at[:, 0], c_sent.at[0])
    wait_for(ids.at[0], c_sent.at[1])
    wait_for(from_core, x_sent)


def step(n, encoded, label_ids, weights, accum):
    labels, width = weights.shape
    vmem = pltpu.VMEM
    dma = pltpu.SemaphoreType.DMA
    results = pl.pallas_call(
        functools.partial(kernel, n),
        out_shape=(
            jax.ShapeDtypeStruct(encoded.shape, BF16),
            jax.ShapeDtypeStruct((labels, width), F32),
            jax.ShapeDtypeStruct((labels, width), F32),
        ),
        in_specs=[
            pl.BlockSpec(memory_space=pltpu.VMEM),
            pl.BlockSpec(memory_space=pltpu.VMEM),
            pl.BlockSpec(memory_space=pltpu.HBM),
            pl.BlockSpec(memory_space=pltpu.HBM),
        ],
        out_specs=(
            pl.BlockSpec(memory_space=pltpu.VMEM),
            pl.BlockSpec(memory_space=pl.ANY),
            pl.BlockSpec(memory_space=pl.ANY),
        ),
        scratch_shapes=[
            vmem((3, 2, n, n, n, 32, 256), BF16),
            vmem((2, n, n, n, 8, 128), jnp.int32),
            vmem((labels, width), F32),
            vmem((3, labels, 256), BF16),
            vmem((2 * n, n * n, 32, 128), jnp.int32),
            vmem((2, 2, n, n, n, 16, labels), BF16),
            vmem((3, 2, 2, n, n, n, 16, 256), BF16),
            vmem((3, 2, n, n, n, 16, 256), BF16),
            vmem((3, 2, n - 1, n, n, 16, 256), BF16),
            vmem((3, 2, n, n, 16, 256), BF16),
            vmem((3, 2, n - 1, n, 16, 256), BF16),
            vmem((3, 2, n, 16, 256), BF16),
            vmem((3, 2, n - 1, 16, 256), BF16),
            vmem((32, 128), jnp.int32),
            vmem((labels, width), F32),
            vmem((3 * (n // 2), n * n * 16, 256), F32),
            dma,
            dma,
            dma,
            dma,
            dma((3,)),
            dma,
            dma((3,)),
            dma((4, 2, 5)),
            dma((2,)),
            dma((4, 2)),
            dma,
            dma((3, 2)),
            dma((3,)),
            dma((3, 3, 2)),
            dma((3,)),
        ],
        compiler_params=pltpu.CompilerParams(
            collective_id=0, has_side_effects=True, vmem_limit_bytes=46 * 2**20
        ),
        name="gradients",
    )(*(pltpu.with_memory_space_constraint(a, pltpu.HBM) for a in (encoded, label_ids, weights, accum)))
    return store(*results)


def store_kernel(pieces, *refs):
    count = len(pieces)
    sources, targets, sems = refs[:count], refs[count : 2 * count], refs[2 * count]
    copies = []
    for source, target, parts in zip(sources, targets, pieces):
        size = source.shape[0] // parts
        for p in range(parts):
            at = pl.ds(p * size, size)
            copies.append(pltpu.make_async_copy(source.at[at], target.at[at], sems.at[len(copies)]))
    for copy in copies:
        copy.start()
    for copy in copies:
        copy.wait()


def store(*arrays):
    pieces = (1, 4, 4)
    return pl.pallas_call(
        functools.partial(store_kernel, pieces),
        out_shape=tuple(jax.ShapeDtypeStruct(a.shape, a.dtype) for a in arrays),
        in_specs=[pl.BlockSpec(memory_space=pltpu.VMEM)] * len(arrays),
        out_specs=(pl.BlockSpec(memory_space=pltpu.HBM),) * len(arrays),
        scratch_shapes=[pltpu.SemaphoreType.DMA((sum(pieces),))],
        compiler_params=pltpu.CompilerParams(vmem_limit_bytes=16 * 2**20),
        name="store",
    )(*arrays)


def solution(mesh):
    n = {4: 2, 32: 4}[mesh.shape["label"]]
    rows = P(("batch", "label"), None)
    return jax.shard_map(
        functools.partial(step, n),
        mesh=mesh,
        in_specs=(rows, rows, rows, rows),
        out_specs=(rows, rows, rows),
        check_vma=False,
    )
```
